32 devices in a mesh: ctx: 16 (over z, x, core), tp: 2 (over y).
Axes of the slice: x: 2, y: 2, z: 4, core: 2. Of those that a mesh axis runs over, the one named last changes fastest.
Arguments:
- queries: bfloat16 [4096, 8192], P('ctx', 'tp'), may hold values from -8 to 8
- key_heads: bfloat16 [4096, 1024], P('ctx', 'tp'), may hold values from -8 to 8
- value_heads: bfloat16 [4096, 1024], P('ctx', 'tp'), may hold values from -6 to 6
- out_grad: bfloat16 [4096, 8192], P(('ctx', 'tp')), may hold values from -6 to 6
- doc_lengths: int32 [8], replicated, may hold values from 1 to 9, 32 in all
Outputs:
- grad_queries: bfloat16 [4096, 8192], P('ctx', 'tp')
- grad_keys: bfloat16 [4096, 1024], P('ctx', 'tp')
- grad_values: bfloat16 [4096, 1024], P('ctx', 'tp')
The draws below stay inside these ranges and needn't reach their ends.
Inputs may be any that keep to these rules, and one draw needn't show every extreme that they name: `doc_lengths`: documents fill the window in order, whole blocks of 128 rows each; the lengths sum to 32 and the longest is exactly 9.
All inputs are finite; a program needn't handle non-finite values.
Results may differ from the reference program's by a relative error of at most 0.009.
Values may be sent and summed in bfloat16 or wider, within the bound.
No kernel may reach another device: no remote copies, remote signals or barrier semaphores. Data moves between devices by JAX's collectives and lax.ppermute only.
A program may use at most 128 MiB of HBM per device.

```python
import math
import jax
import jax.numpy as jnp
import numpy as np
from jax import lax

HD = 128
QH = 64
KVH = 8
GROUP = 8
BLK = 128
TOKENS = 4096
NBLK = 32
MAXDOC = 9
NDOCS = 8


def draw_queries(key, part):
    base = jnp.clip(jax.random.normal(jax.random.fold_in(key, 1), (TOKENS, QH * HD), jnp.float32), -6.0, 6.0)
    return base.astype(jnp.bfloat16)


def draw_key_heads(key, part):
    base = jnp.clip(jax.random.normal(jax.random.fold_in(key, 2), (TOKENS, KVH * HD), jnp.float32), -6.0, 6.0)
    return base.astype(jnp.bfloat16)


def levels(rng, shape, shards, low, largest):
    gain, own = 1.0, jax.random.fold_in(rng, 6)
    for axis_at, shards_of in shards:
        heights = jnp.exp(jax.random.uniform(jax.random.fold_in(own, axis_at), (shards_of,), jnp.float32, low / len(shards), largest / len(shards)))
        gain = gain * jnp.repeat(heights, shape[axis_at] // shards_of).reshape([-1 if axis == axis_at else 1 for axis in range(len(shape))])
    return gain


def split_up(amount, total, bound, lean):
    portions = [(1 << 20) // math.isqrt(standing ** lean) + 1 for standing in range(2, amount + 1)]
    rest, given = total - bound - (amount - 1), [1] * (amount - 1)
    while rest > 0:
        free = [i for i in range(amount - 1) if given[i] < bound]
        pool, remaining = sum([portions[i] for i in free]), rest
        for i in free:
            more = min(bound - given[i], max(1, remaining * portions[i] // pool), rest)
            given[i] = given[i] + more
            rest = rest - more
    return np.array([bound] + given)


def uneven(key, amount, total, limit, slope):
    if amount == 2:
        one = jax.random.randint(key, (), max(1, total - limit), min(limit, total - 1) + 1)
        return jnp.stack([one, total - one])
    tallies = jnp.asarray(split_up(amount, total, limit, slope), jnp.int32)
    couples = (amount - 1) // 2
    donor, taker = tallies[1:1 + 2 * couples:2], tallies[2:2 + 2 * couples:2]
    slack = jnp.minimum(donor - 1, limit - taker)
    moved = jax.random.randint(jax.random.fold_in(key, 1), (couples,), 0, 1 << 20) % (slack + 1)
    tallies = tallies.at[1:1 + 2 * couples:2].set(donor - moved).at[2:2 + 2 * couples:2].set(taker + moved)
    return tallies[jax.random.permutation(jax.random.fold_in(key, 2), amount)]


def centred(own_key, extent, scale, reach, pieces=(), kind=jnp.bfloat16):
    array = scale * jax.random.normal(own_key, extent, jnp.float32)
    if pieces:
        array = array * levels(own_key, extent, pieces, -0.22, 0.18)
    return jnp.clip(array, -reach, reach).astype(kind)


def setup_inputs(seed: int = 0) -> dict:
    key_of = jax.random.split(jax.random.key(seed), 6)
    queries = draw_queries(jax.random.fold_in(key_of[5], 71), 0)
    key_heads = draw_key_heads(jax.random.fold_in(key_of[5], 71), 0)
    value_heads = centred(key_of[2], (TOKENS, KVH * HD), 1.0, 6.0, ((0, 16), (1, 2)))
    out_grad = centred(key_of[3], (TOKENS, QH * HD), 1.0, 6.0, ((0, 32),))
    doc_lengths = uneven(key_of[4], NDOCS, NBLK, MAXDOC, 2).astype(jnp.int32)
    return {"queries": queries, "key_heads": key_heads, "value_heads": value_heads, "out_grad": out_grad, "doc_lengths": doc_lengths}


def doc_index(rows, doc_ends):
    return jnp.sum((rows[:, None] >= doc_ends[None, :]).astype(jnp.int32), axis=1)


def reference(queries, key_heads, value_heads, out_grad, doc_lengths):
    score_scale = HD ** -0.5
    window = MAXDOC * BLK
    behind = (MAXDOC - 1) * BLK
    doc_ends = jnp.cumsum(doc_lengths).astype(jnp.int32) * BLK
    padding = jnp.zeros((behind, KVH * HD), jnp.bfloat16)
    keys_pad = jnp.concatenate([padding, key_heads], axis=0)
    values_pad = jnp.concatenate([padding, value_heads], axis=0)
    offsets = jnp.arange(BLK, dtype=jnp.int32)
    spread = jnp.arange(window, dtype=jnp.int32)
    highest = lax.Precision.HIGHEST

    def block_step(state, block_id):
        grad_k, grad_v = state
        start_row = (block_id * BLK).astype(jnp.int32)
        query_rows = start_row + offsets
        key_rows = start_row - behind + spread
        allowed = (doc_index(query_rows, doc_ends)[:, None] == doc_index(key_rows, doc_ends)[None, :]) & (key_rows[None, :] <= query_rows[:, None]) & (key_rows[None, :] >= 0)
        query_block = lax.dynamic_slice_in_dim(queries, start_row, BLK, 0).astype(jnp.float32).reshape(BLK, KVH, GROUP, HD)
        grad_block = lax.dynamic_slice_in_dim(out_grad, start_row, BLK, 0).astype(jnp.float32).reshape(BLK, KVH, GROUP, HD)
        key_block = lax.dynamic_slice_in_dim(keys_pad, start_row, window, 0).astype(jnp.float32).reshape(window, KVH, HD)
        value_block = lax.dynamic_slice_in_dim(values_pad, start_row, window, 0).astype(jnp.float32).reshape(window, KVH, HD)
        scores = jnp.einsum("rkgd,ckd->kgrc", query_block, key_block, precision=highest)
        scores = jnp.where(allowed, scores * score_scale, -jnp.inf)
        row_max = jnp.max(scores, axis=-1)
        row_sum = jnp.sum(jnp.exp(scores - row_max[..., None]), axis=-1)
        log_total = row_max + jnp.log(row_sum)
        weights = jnp.exp(scores - log_total[..., None])
        grad_prob = jnp.einsum("rkgd,ckd->kgrc", grad_block, value_block, precision=highest)
        grad_dot = jnp.sum(weights * grad_prob, axis=-1)
        rounded = lax.optimization_barrier(weights.astype(jnp.bfloat16)).astype(jnp.float32)
        value_term = jnp.einsum("kgrc,rkgd->ckd", rounded, grad_block, precision=highest).reshape(window, KVH * HD)
        dscore = lax.optimization_barrier((weights * (grad_prob - grad_dot[..., None])).astype(jnp.bfloat16)).astype(jnp.float32)
        query_term = jnp.einsum("kgrc,ckd->rkgd", dscore, key_block, precision=highest) * score_scale
        key_term = jnp.einsum("kgrc,rkgd->ckd", dscore, query_block, precision=highest).reshape(window, KVH * HD) * score_scale
        grad_k = lax.dynamic_update_slice_in_dim(grad_k, lax.dynamic_slice_in_dim(grad_k, start_row, window, 0) + key_term, start_row, 0)
        grad_v = lax.dynamic_update_slice_in_dim(grad_v, lax.dynamic_slice_in_dim(grad_v, start_row, window, 0) + value_term, start_row, 0)
        return (grad_k, grad_v), query_term.reshape(BLK, QH * HD).astype(jnp.bfloat16)

    zero_pad = jnp.zeros((TOKENS + behind, KVH * HD), jnp.float32)
    (grad_k, grad_v), grad_q = lax.scan(block_step, (zero_pad, zero_pad), jnp.arange(NBLK, dtype=jnp.int32))
    return (grad_q.reshape(TOKENS, QH * HD), grad_k[behind:].astype(jnp.bfloat16), grad_v[behind:].astype(jnp.bfloat16))
```

```python
import functools
import math

import jax
import jax.numpy as jnp
from jax import lax
from jax.experimental import pallas as pl
from jax.experimental.pallas import tpu as pltpu
from jax.sharding import PartitionSpec as P

HD = 128
GROUP = 8
BLK = 128
MAXDOC = 9
REACH = 4
GW = GROUP * HD
SCALE = HD ** (-0.5)
EXP2_SCALE = SCALE * math.log2(math.e)
CHUNKS = (4,)
HEADS_AT_ONCE = 8


def passed_along(block, axis, distance):
    devices = range(lax.axis_size(axis))
    route = [(i - distance, i) for i in devices if i - distance in devices]
    return lax.ppermute(block, axis, route)


def attention_grads(docs, where, q_ref, do_refs, k_refs, v_refs, dq_ref, own_ref, part_refs, scratch):
    keys, values, grads, dk_sum, dv_sum = scratch
    rows = q_ref.shape[0]
    blocks = rows // BLK
    back = REACH * rows
    ctx, tp = where[0], where[1]
    for distance in range(REACH + 1):
        at = pl.ds((REACH - distance) * rows, rows)
        keys[at, :] = k_refs[distance][...]
        values[at, :] = v_refs[distance][...]
    if len(do_refs) == 1:
        grads[...] = do_refs[0][...]
    else:
        half = rows // 2
        grads[pl.ds(pl.multiple_of(tp * half, half), half), :] = do_refs[0][...]
        grads[pl.ds(pl.multiple_of((1 - tp) * half, half), half), :] = do_refs[1][...]
    dk_sum[...] = jnp.zeros_like(dk_sum)
    dv_sum[...] = jnp.zeros_like(dv_sum)
    width = HEADS_AT_ONCE * BLK

    def row_block(block, count):
        first = pl.multiple_of(block * BLK, BLK)
        reach = pl.ds(pl.multiple_of(back + first - (count - 1) * BLK, BLK), count * BLK)
        here = pl.ds(first, BLK)
        key_block = keys[reach, :]
        value_block = values[reach, :]
        key_row = lax.broadcasted_iota(jnp.int32, (BLK, width), 0)
        query_row = lax.broadcasted_iota(jnp.int32, (BLK, width), 1) & (BLK - 1)
        visible = key_row <= query_row
        for first_head in range(0, GROUP, HEADS_AT_ONCE):
            heads = range(first_head, first_head + HEADS_AT_ONCE)
            query = jnp.concatenate([q_ref[here, pl.ds(h * HD, HD)] for h in heads], axis=0)
            grad = jnp.concatenate([grads[here, pl.ds(h * HD, HD)] for h in heads], axis=0)
            turned = (((1,), (1,)), ((), ()))
            scores = lax.dot_general(key_block, query, turned, preferred_element_type=jnp.float32)
            dprob = lax.dot_general(value_block, grad, turned, preferred_element_type=jnp.float32)
            last = jnp.where(visible, scores[(count - 1) * BLK :, :], -jnp.inf)
            if count > 1:
                scores = jnp.concatenate([scores[: (count - 1) * BLK, :], last], axis=0)
            else:
                scores = last
            top = jnp.max(scores, axis=0, keepdims=True)
            lifted = jnp.exp2(scores * EXP2_SCALE - top * EXP2_SCALE)
            inverse = 1.0 / jnp.sum(lifted, axis=0, keepdims=True)
            delta = jnp.sum(lifted * dprob, axis=0, keepdims=True) * inverse
            prob = lifted * inverse
            dscore = (prob * (dprob - delta)).astype(jnp.bfloat16)
            dv_sum[reach, :] += jnp.dot(
                prob.astype(jnp.bfloat16), grad, preferred_element_type=jnp.float32
            )
            dk_sum[reach, :] += jnp.dot(dscore, query, preferred_element_type=jnp.float32)
            first_dims = (((0,), (0,)), ((), ()))
            dquery = lax.dot_general(
                key_block, dscore, first_dims, preferred_element_type=jnp.float32
            ).T
            dquery = (dquery * SCALE).astype(jnp.bfloat16)
            for n, h in enumerate(heads):
                dq_ref[here, pl.ds(h * HD, HD)] = dquery[n * BLK : (n + 1) * BLK, :]

    def visit(block, carry):
        index = ctx * blocks + block

        def seek(k, state):
            end, start = state
            end = end + docs[k]
            return end, jnp.where(end <= index, end, start)

        _, start = lax.fori_loop(0, docs.shape[0], seek, (0, 0))
        for count in range(1, MAXDOC + 1):
            pl.when(index - start == count - 1)(functools.partial(row_block, block, count))
        return carry

    lax.fori_loop(0, blocks, visit, 0)
    for distance in range(REACH + 1):
        at = pl.ds((REACH - distance) * rows, rows)
        target = own_ref if distance == 0 else part_refs[distance - 1]
        target[:, :HD] = (dk_sum[at, :] * SCALE).astype(target.dtype)
        target[:, HD:] = dv_sum[at, :].astype(target.dtype)


def chunk_call(docs, where, queries, out_grad, peer, own_k, own_v, passed, dq_so_far, first, count):
    rows = queries.shape[0]
    pairs = queries.shape[1] // GW
    back = REACH * rows

    def body(*refs):
        docs_ref, where_ref, refs = refs[0], refs[1], list(refs[2:])
        q_ref = refs.pop(0)
        do_refs = [refs.pop(0) for _ in range(1 if peer is None else 2)]
        k_refs = [refs.pop(0) for _ in range(REACH + 1)]
        v_refs = [refs.pop(0) for _ in range(REACH + 1)]
        if dq_so_far is not None:
            refs.pop(0)
        dq_ref, own_ref = refs.pop(0), refs.pop(0)
        part_refs = [refs.pop(0) for _ in range(REACH)]
        attention_grads(
            docs_ref, where_ref, q_ref, do_refs, k_refs, v_refs, dq_ref, own_ref, part_refs, refs
        )

    wide = pl.BlockSpec((rows, GW), lambda j, docs, where: (0, first + j))
    if peer is None:
        gives = [out_grad]
        give_specs = [wide]
    else:
        gives = [out_grad, peer]
        give_specs = [
            pl.BlockSpec((rows // 2, GW), lambda j, docs, where: (0, where[1] * pairs + first + j)),
            pl.BlockSpec((rows // 2, GW), lambda j, docs, where: (0, j)),
        ]
    own_spec = pl.BlockSpec((rows, HD), lambda j, docs, where: (0, first + j))
    k_spec = pl.BlockSpec((rows, HD), lambda j, docs, where: (0, 2 * j))
    v_spec = pl.BlockSpec((rows, HD), lambda j, docs, where: (0, 2 * j + 1))
    pair_spec = pl.BlockSpec((rows, 2 * HD), lambda j, docs, where: (0, j))
    operands = [docs, where, queries, *gives, own_k, *passed, own_v, *passed]
    in_specs = [wide, *give_specs, own_spec, *[k_spec] * REACH, own_spec, *[v_spec] * REACH]
    aliases = {}
    if dq_so_far is not None:
        aliases = {len(operands): 0}
        operands.append(dq_so_far)
        in_specs.append(pl.BlockSpec(memory_space=pl.ANY))
    pair_shape = (rows, 2 * HD * count)
    flops = 5 * 2 * (2 * 5 * BLK) * (rows * GROUP) * HD * count
    return pl.pallas_call(
        body,
        grid_spec=pltpu.PrefetchScalarGridSpec(
            num_scalar_prefetch=2,
            grid=(count,),
            in_specs=in_specs,
            out_specs=[wide, pair_spec, *[pair_spec] * REACH],
            scratch_shapes=[
                pltpu.VMEM((back + rows, HD), jnp.bfloat16),
                pltpu.VMEM((back + rows, HD), jnp.bfloat16),
                pltpu.VMEM((rows, GW), jnp.bfloat16),
                pltpu.VMEM((back + rows, HD), jnp.float32),
                pltpu.VMEM((back + rows, HD), jnp.float32),
            ],
        ),
        out_shape=[
            jax.ShapeDtypeStruct(queries.shape, jnp.bfloat16),
            jax.ShapeDtypeStruct(pair_shape, jnp.float32),
            *[jax.ShapeDtypeStruct(pair_shape, jnp.bfloat16)] * REACH,
        ],
        input_output_aliases=aliases,
        compiler_params=pltpu.CompilerParams(vmem_limit_bytes=48 * 2**20),
        cost_estimate=pl.CostEstimate(
            flops=flops, bytes_accessed=4 * rows * GW * 2 * count, transcendentals=0
        ),
        name="attention_grads",
    )(*operands)


def add_up(own, arrived):
    rows = own[0].shape[0]
    widths = [a.shape[1] for a in own]
    total = sum(widths) // 2

    def body(*refs):
        key_ref, value_ref = refs[-2:]
        at = 0
        for c, width in enumerate(widths):
            mine = refs[c * (REACH + 1)]
            others = refs[c * (REACH + 1) + 1 : (c + 1) * (REACH + 1)]
            for j in range(width // (2 * HD)):
                for half, target in enumerate((key_ref, value_ref)):
                    cols = pl.ds((2 * j + half) * HD, HD)
                    value = mine[:, cols]
                    for other in others:
                        value = value + other[:, cols].astype(jnp.float32)
                    target[:, pl.ds(at + j * HD, HD)] = value.astype(jnp.bfloat16)
            at += width // 2

    operands = []
    for c in range(len(own)):
        operands += [own[c], *arrived[c]]
    return pl.pallas_call(
        body,
        out_shape=[jax.ShapeDtypeStruct((rows, total), jnp.bfloat16)] * 2,
        compiler_params=pltpu.CompilerParams(vmem_limit_bytes=48 * 2**20),
        name="add_up",
    )(*operands)


def body(queries, key_heads, value_heads, out_grad, doc_lengths):
    pairs = key_heads.shape[1] // HD
    tp = lax.axis_index("tp")
    where = jnp.stack([lax.axis_index("ctx"), tp]).astype(jnp.int32)
    swap = lax.axis_size("tp") == 2
    if not swap:
        out_grad = lax.all_to_all(out_grad, "tp", split_axis=1, concat_axis=0, tiled=True)
    sizes = CHUNKS if sum(CHUNKS) == pairs else (1,) * pairs
    first = 0
    dq = None
    own, arrived = [], []
    inputs = []
    for size in sizes:
        peer = None
        if swap:
            at = (1 - tp) * (pairs * GW) + first * GW
            leaving = lax.dynamic_slice_in_dim(out_grad, at, size * GW, 1)
            peer = lax.ppermute(leaving, "tp", [(0, 1), (1, 0)])
        cols = [slice((first + j) * HD, (first + j + 1) * HD) for j in range(size)]
        packed = jnp.concatenate([a[:, c] for c in cols for a in (key_heads, value_heads)], axis=1)
        passed = [passed_along(packed, "ctx", d) for d in range(1, REACH + 1)]
        inputs.append((peer, passed, first, size))
        first += size
    for peer, passed, first, size in inputs:
        dq, mine, *parts = chunk_call(
            doc_lengths, where, queries, out_grad, peer, key_heads, value_heads, passed, dq, first, size
        )
        own.append(mine)
        arrived.append([passed_along(parts[d - 1], "ctx", -d) for d in range(1, REACH + 1)])
    key_total, value_total = add_up(own, arrived)
    return dq, key_total, value_total


def solution(mesh):
    placed = (P("ctx", "tp"), P("ctx", "tp"), P("ctx", "tp"), P(("ctx", "tp"), None), P())
    return jax.shard_map(
        body,
        mesh=mesh,
        in_specs=placed,
        out_specs=(P("ctx", "tp"), P("ctx", "tp"), P("ctx", "tp")),
        check_vma=False,
    )
```

```python
import functools
import math

import jax
import jax.numpy as jnp
from jax import lax
from jax.experimental import pallas as pl
from jax.experimental.pallas import tpu as pltpu
from jax.sharding import PartitionSpec as P

HD = 128
GROUP = 8
BLK = 128
MAXDOC = 9
REACH = 4
GW = GROUP * HD
SCALE = HD ** (-0.5)
EXP2_SCALE = SCALE * math.log2(math.e)
CHUNKS = (2, 2)
HEADS_AT_ONCE = 4
LOWEST = -1e30
PREPARE_VMEM = 60 * 2**20
VARIANTS = (2, 4, 6, 8, 9)


def passed_along(block, axis, distance):
    devices = range(lax.axis_size(axis))
    route = [(i - distance, i) for i in devices if i - distance in devices]
    return lax.ppermute(block, axis, route)


def attention_grads(docs, where, q_ref, do_refs, k_refs, v_refs, dq_ref, own_ref, part_refs, scratch):
    keys, values, grads, dk_sum, dv_sum = scratch
    rows = q_ref.shape[0]
    blocks = rows // BLK
    back = REACH * rows
    ctx, tp = where[0], where[1]
    for distance in range(REACH + 1):
        at = pl.ds((REACH - distance) * rows, rows)
        keys[at, :] = k_refs[distance][...]
        values[at, :] = v_refs[distance][...]
    if len(do_refs) == 1:
        grads[...] = do_refs[0][...]
    else:
        half = rows // 2
        grads[pl.ds(pl.multiple_of(tp * half, half), half), :] = do_refs[0][...]
        for j, peer_ref in enumerate(do_refs[1:]):

            @pl.when(pl.program_id(0) == j)
            def take(peer_ref=peer_ref):
                grads[pl.ds(pl.multiple_of((1 - tp) * half, half), half), :] = peer_ref[...]

    dk_sum[...] = jnp.zeros_like(dk_sum)
    dv_sum[...] = jnp.zeros_like(dv_sum)
    width = HEADS_AT_ONCE * BLK
    groups = GROUP // HEADS_AT_ONCE
    turned = (((1,), (1,)), ((), ()))
    first_dims = (((0,), (0,)), ((), ()))

    def row_block(block, count, least, needed):
        first = pl.multiple_of(block * BLK, BLK)
        here = pl.ds(first, BLK)
        reach_at = back + first - (count - 1) * BLK
        key_row = lax.broadcasted_iota(jnp.int32, (BLK, width), 0)
        query_row = lax.broadcasted_iota(jnp.int32, (BLK, width), 1) & (BLK - 1)
        visible = key_row <= query_row

        def reach(n, length=1):
            return pl.ds(pl.multiple_of(reach_at + n * BLK, BLK), length * BLK)

        def load(group):
            cols = [pl.ds((group * HEADS_AT_ONCE + i) * HD, HD) for i in range(HEADS_AT_ONCE)]
            query = jnp.concatenate([q_ref[here, c] for c in cols], axis=0)
            grad = jnp.concatenate([grads[here, c] for c in cols], axis=0)
            return cols, query, grad

        def block_stats(loaded, n):
            _, query, grad = loaded
            scores = lax.dot_general(
                keys[reach(n), :], query, turned, preferred_element_type=jnp.float32
            )
            dprob = lax.dot_general(
                values[reach(n), :], grad, turned, preferred_element_type=jnp.float32
            )
            if n == count - 1:
                scores = jnp.where(visible, scores, -jnp.inf)
            top = jnp.max(scores, axis=0, keepdims=True)
            if n < count - least:
                kept = n >= count - needed
                top = jnp.where(kept, top, LOWEST)
                lifted = jnp.where(kept, jnp.exp2(scores * EXP2_SCALE - top * EXP2_SCALE), 0.0)
            else:
                lifted = jnp.exp2(scores * EXP2_SCALE - top * EXP2_SCALE)
            total = jnp.sum(lifted, axis=0, keepdims=True)
            dot = jnp.sum(lifted * dprob, axis=0, keepdims=True)
            return lifted, dprob, top, total, dot

        def combine(parts):
            top = functools.reduce(jnp.maximum, [p[2] for p in parts])
            weights = [jnp.exp2((p[2] - top) * EXP2_SCALE) for p in parts]
            inverse = 1.0 / sum(p[3] * w for p, w in zip(parts, weights))
            delta = sum(p[4] * w for p, w in zip(parts, weights)) * inverse
            return [w * inverse for w in weights], delta

        def block_grads(loaded, n, part, weight, delta):
            _, query, grad = loaded
            prob = part[0] * weight
            dscore = (prob * (part[1] - delta)).astype(jnp.bfloat16)
            dv_sum[reach(n), :] += jnp.dot(
                prob.astype(jnp.bfloat16), grad, preferred_element_type=jnp.float32
            )
            dk_sum[reach(n), :] += jnp.dot(dscore, query, preferred_element_type=jnp.float32)
            return dscore

        loaded = load(0)
        parts = [block_stats(loaded, n) for n in range(count)]
        for group in range(groups):
            weights, delta = combine(parts)
            later = load(group + 1) if group + 1 < groups else None
            later_parts, dscores = [], []
            for n in range(count):
                if later is not None:
                    later_parts.append(block_stats(later, n))
                dscores.append(block_grads(loaded, n, parts[n], weights[n], delta))
            dscore = jnp.concatenate(dscores, axis=0) if count > 1 else dscores[0]
            dquery = lax.dot_general(
                keys[reach(0, count), :], dscore, first_dims, preferred_element_type=jnp.float32
            ).T
            dquery = (dquery * SCALE).astype(jnp.bfloat16)
            for i, c in enumerate(loaded[0]):
                dq_ref[here, c] = dquery[i * BLK : (i + 1) * BLK, :]
            loaded, parts = later, later_parts

    def visit(block, carry):
        index = ctx * blocks + block

        def seek(k, state):
            end, start = state
            end = end + docs[k]
            return end, jnp.where(end <= index, end, start)

        _, start = lax.fori_loop(0, docs.shape[0], seek, (0, 0))
        needed = index - start + 1
        least = 1
        for count in VARIANTS:
            pl.when((needed >= least) & (needed <= count))(
                functools.partial(row_block, block, count, least, needed)
            )
            least = count + 1
        return carry

    lax.fori_loop(0, blocks, visit, 0)
    for distance in range(REACH + 1):
        at = pl.ds((REACH - distance) * rows, rows)
        if distance % 2:
            target, to = part_refs[0], pl.ds((distance // 2) * rows, rows)
        else:
            target, to = (own_ref, *part_refs[1:])[distance // 2], pl.ds(0, rows)
        target[to, :HD] = (dk_sum[at, :] * SCALE).astype(target.dtype)
        target[to, HD:] = dv_sum[at, :].astype(target.dtype)


def chunk_call(
    docs, where, queries, out_grad, peer, own_k, own_v, even, odd, dq_so_far, first, count
):
    rows = queries.shape[0]
    pairs = queries.shape[1] // GW
    back = REACH * rows

    def body(*refs):
        docs_ref, where_ref, refs = refs[0], refs[1], list(refs[2:])
        q_ref = refs.pop(0)
        do_refs = [refs.pop(0) for _ in range(1 if peer is None else 1 + count)]
        k_refs = [refs.pop(0) for _ in range(REACH + 1)]
        v_refs = [refs.pop(0) for _ in range(REACH + 1)]
        if dq_so_far is not None:
            refs.pop(0)
        dq_ref, own_ref = refs.pop(0), refs.pop(0)
        part_refs = [refs.pop(0) for _ in range(3)]
        attention_grads(
            docs_ref, where_ref, q_ref, do_refs, k_refs, v_refs, dq_ref, own_ref, part_refs, refs
        )

    wide = pl.BlockSpec((rows, GW), lambda j, docs, where: (0, first + j))
    if peer is None:
        gives = [out_grad]
        give_specs = [wide]
    else:
        gives = [out_grad, *peer]
        give_specs = [
            pl.BlockSpec((rows // 2, GW), lambda j, docs, where: (0, where[1] * pairs + first + j)),
            *[pl.BlockSpec((rows // 2, GW), lambda j, docs, where: (0, 0))] * count,
        ]
    own_spec = pl.BlockSpec((rows, HD), lambda j, docs, where: (0, first + j))
    k_specs, v_specs = [own_spec], [own_spec]
    for distance in range(1, REACH + 1):
        row = distance // 2 if distance % 2 else 0
        k_specs.append(pl.BlockSpec((rows, HD), lambda j, docs, where, row=row: (row, 2 * j)))
        v_specs.append(pl.BlockSpec((rows, HD), lambda j, docs, where, row=row: (row, 2 * j + 1)))
    passed = [odd, even[0], odd, even[1]]
    pair_spec = pl.BlockSpec((rows, 2 * HD), lambda j, docs, where: (0, j))
    operands = [docs, where, queries, *gives, own_k, *passed, own_v, *passed]
    in_specs = [wide, *give_specs, *k_specs, *v_specs]
    aliases = {}
    if dq_so_far is not None:
        aliases = {len(operands): 0}
        operands.append(dq_so_far)
        in_specs.append(pl.BlockSpec(memory_space=pl.ANY))
    pair_shape = (rows, 2 * HD * count)
    both_spec = pl.BlockSpec((2 * rows, 2 * HD), lambda j, docs, where: (0, j))
    both_shape = (2 * rows, 2 * HD * count)
    flops = 5 * 2 * (2 * 5 * BLK) * (rows * GROUP) * HD * count
    return pl.pallas_call(
        body,
        grid_spec=pltpu.PrefetchScalarGridSpec(
            num_scalar_prefetch=2,
            grid=(count,),
            in_specs=in_specs,
            out_specs=[wide, pair_spec, both_spec, pair_spec, pair_spec],
            scratch_shapes=[
                pltpu.VMEM((back + rows, HD), jnp.bfloat16),
                pltpu.VMEM((back + rows, HD), jnp.bfloat16),
                pltpu.VMEM((rows, GW), jnp.bfloat16),
                pltpu.VMEM((back + rows, HD), jnp.float32),
                pltpu.VMEM((back + rows, HD), jnp.float32),
            ],
        ),
        out_shape=[
            jax.ShapeDtypeStruct(queries.shape, jnp.bfloat16),
            jax.ShapeDtypeStruct(pair_shape, jnp.float32),
            jax.ShapeDtypeStruct(both_shape, jnp.bfloat16),
            *[jax.ShapeDtypeStruct(pair_shape, jnp.bfloat16)] * 2,
        ],
        input_output_aliases=aliases,
        compiler_params=pltpu.CompilerParams(vmem_limit_bytes=48 * 2**20),
        cost_estimate=pl.CostEstimate(
            flops=flops, bytes_accessed=4 * rows * GW * 2 * count, transcendentals=0
        ),
        name="attention_grads",
    )(*operands)


def add_up(where, own, crossed, arrived):
    rows = own[0].shape[0]
    widths = [a.shape[1] for a in own]
    total = sum(widths) // 2

    def body(where_ref, *refs):
        key_ref, value_ref = refs[-2:]
        first_core = where_ref[0] % 2 == 0
        at = 0
        for c, width in enumerate(widths):
            mine, over, two, four = refs[4 * c : 4 * c + 4]
            for j in range(width // (2 * HD)):
                for half, target in enumerate((key_ref, value_ref)):
                    cols = pl.ds((2 * j + half) * HD, HD)
                    near = over[pl.ds(0, rows), cols].astype(jnp.float32)
                    value = mine[:, cols] + jnp.where(first_core, near, 0.0)
                    value = value + two[:, cols].astype(jnp.float32)
                    value = value + four[:, cols].astype(jnp.float32)
                    target[:, pl.ds(at + j * HD, HD)] = value.astype(jnp.bfloat16)
            at += width // 2

    operands = []
    for c in range(len(own)):
        operands += [own[c], crossed[c], *arrived[c]]
    vmem = pl.BlockSpec(memory_space=pltpu.VMEM)
    return pl.pallas_call(
        body,
        in_specs=[pl.BlockSpec(memory_space=pltpu.SMEM)] + [vmem] * len(operands),
        out_specs=[vmem, vmem],
        out_shape=[jax.ShapeDtypeStruct((rows, total), jnp.bfloat16)] * 2,
        compiler_params=pltpu.CompilerParams(vmem_limit_bytes=48 * 2**20),
        name="add_up",
    )(where, *operands)


def prepare(where, key_heads, value_heads, out_grad, first, size, swap):
    rows = key_heads.shape[0]
    pairs = key_heads.shape[1] // HD

    def body(where_ref, k_ref, v_ref, *refs):
        packed_ref = refs[1 if swap else 0]
        for j in range(size):
            cols = pl.ds(j * HD, HD)
            packed_ref[:, pl.ds(2 * j * HD, HD)] = k_ref[:, cols]
            packed_ref[:, pl.ds((2 * j + 1) * HD, HD)] = v_ref[:, cols]
        if swap:
            for j in range(size):
                refs[2 + j][...] = refs[0][:, pl.ds(j * GW, GW)]

    pair_spec = pl.BlockSpec((rows, size * HD), lambda i, where: (0, first // size))
    in_specs, operands = [pair_spec, pair_spec], [key_heads, value_heads]
    out_shape = [jax.ShapeDtypeStruct((rows, 2 * HD * size), jnp.bfloat16)]
    out_specs = [pl.BlockSpec((rows, 2 * HD * size), lambda i, where: (0, 0))]
    if swap:
        at = pairs // size
        in_specs.append(
            pl.BlockSpec(
                (rows // 2, size * GW), lambda i, where: (0, (1 - where[1]) * at + first // size)
            )
        )
        operands.append(out_grad)
        for _ in range(size):
            out_shape.append(jax.ShapeDtypeStruct((rows // 2, GW), jnp.bfloat16))
            out_specs.append(pl.BlockSpec((rows // 2, GW), lambda i, where: (0, 0)))
    return pl.pallas_call(
        body,
        grid_spec=pltpu.PrefetchScalarGridSpec(
            num_scalar_prefetch=1, grid=(1,), in_specs=in_specs, out_specs=out_specs
        ),
        out_shape=out_shape,
        compiler_params=pltpu.CompilerParams(vmem_limit_bytes=PREPARE_VMEM),
        name="prepare",
    )(where, *operands)


def swapped(block, step):
    return lax.ppermute(block, "ctx", [(i, i ^ step) for i in range(lax.axis_size("ctx"))])


def body(queries, key_heads, value_heads, out_grad, doc_lengths):
    pairs = key_heads.shape[1] // HD
    ctx = lax.axis_index("ctx")
    where = jnp.stack([ctx, lax.axis_index("tp")]).astype(jnp.int32)
    first_core = ctx % 2 == 0
    first_chip = ctx % 4 < 2
    swap = lax.axis_size("tp") == 2
    if not swap:
        out_grad = lax.all_to_all(out_grad, "tp", split_axis=1, concat_axis=0, tiled=True)
    sizes = CHUNKS if sum(CHUNKS) == pairs else (1,) * pairs
    first = 0
    dq = None
    own, crossed, arrived, inputs = [], [], [], []
    packs, peers, fours, twos = [], [], [], []
    for size in sizes:
        packed, *leaving = prepare(where, key_heads, value_heads, out_grad, first, size, swap)
        packs.append(packed)
        peers.append([lax.ppermute(g, "tp", [(0, 1), (1, 0)]) for g in leaving])
        fours.append(passed_along(packed, "ctx", 4))
        first += size
    first = 0
    for c, size in enumerate(sizes):
        packed, four = packs[c], fours[c]
        if swap and c == 0:
            four, peers[c][0] = lax.optimization_barrier((four, peers[c][0]))
        two = swapped(jnp.where(first_chip, packed, four), 2)
        if swap and c == 0:
            two, peers[c], fours[1:] = lax.optimization_barrier((two, peers[c], fours[1:]))
        near = jnp.where(first_core, packed, two)
        far = jnp.where(first_core, two, four)
        odd = swapped(jnp.concatenate([near, far], axis=0), 1)
        inputs.append((peers[c] if swap else None, (two, four), odd, first, size))
        first += size
    sent = None
    for c, (peer, even, odd, first, size) in enumerate(inputs):
        if sent is not None:
            dq, sent = lax.optimization_barrier((dq, sent))
            arrived.append([passed_along(sent[0], "ctx", -2), passed_along(sent[1], "ctx", -4)])
        dq, mine, one_three, two, four = chunk_call(
            doc_lengths, where, queries, out_grad, peer, key_heads, value_heads, even, odd, dq, first, size
        )
        if swap and c + 1 < len(sizes):
            one_three, peers[c + 1][:] = lax.optimization_barrier((one_three, peers[c + 1]))
        if arrived:
            one_three, arrived[-1] = lax.optimization_barrier((one_three, arrived[-1]))
        over = swapped(one_three, 1)
        rows = mine.shape[0]
        near, far = over[:rows].astype(jnp.float32), over[rows:].astype(jnp.float32)
        two = (two.astype(jnp.float32) + jnp.where(first_core, far, near)).astype(jnp.bfloat16)
        four = (four.astype(jnp.float32) + jnp.where(first_core, 0.0, far)).astype(jnp.bfloat16)
        own.append(mine)
        crossed.append(over)
        sent = (two, four)
    arrived.append([passed_along(sent[0], "ctx", -2), passed_along(sent[1], "ctx", -4)])
    key_total, value_total = add_up(where, own, crossed, arrived)
    return dq, key_total, value_total


def solution(mesh):
    placed = (P("ctx", "tp"), P("ctx", "tp"), P("ctx", "tp"), P(("ctx", "tp"), None), P())
    return jax.shard_map(
        body,
        mesh=mesh,
        in_specs=placed,
        out_specs=(P("ctx", "tp"), P("ctx", "tp"), P("ctx", "tp")),
        check_vma=False,
    )
```
